32 devices in a mesh: section: 2 (over core), ctx: 4 (over z), tensor: 4 (over y, x).
Axes of the slice: x: 2, y: 2, z: 4, core: 2. Of those that a mesh axis runs over, the one named last changes fastest.
Arguments:
- boundary_in: bfloat16 [2, 4, 1024, 768], P('section', None, 'ctx'), may hold values from -6 to 6
- segments: int32 [4, 1024], replicated, may hold values from 0 to 2, never falling along the last dimension, each value on 1 to 512 neighbouring positions
- ln1_gain: bfloat16 [2, 768], P('section', 'ctx'), may hold values from 0.5 to 1.5
- ln1_bias: bfloat16 [2, 768], P('section', 'ctx'), may hold values from -2 to 2
- w_qkv: bfloat16 [2, 3, 768, 768], P('section', None, 'ctx', 'tensor'), may hold values from -0.21875 to 0.21875
- b_qv: bfloat16 [2, 2, 768], P('section', None, 'tensor'), may hold values from -0.29882812 to 0.29882812
- w_out: bfloat16 [2, 768, 768], P('section', 'tensor', 'ctx'), may hold values from -3 to 3
- b_out: bfloat16 [2, 768], P('section', 'ctx'), may hold values from -3 to 3
- ln2_gain: bfloat16 [2, 768], P('section', 'ctx'), may hold values from 0.5 to 1.5
- ln2_bias: bfloat16 [2, 768], P('section', 'ctx'), may hold values from -2 to 2
- w_up: bfloat16 [2, 768, 3072], P('section', 'ctx', 'tensor'), may hold values from -0.21875 to 0.21875
- b_up: bfloat16 [2, 3072], P('section', 'tensor'), may hold values from -3 to 3
- w_down: bfloat16 [2, 3072, 768], P('section', 'tensor', 'ctx'), may hold values from -0.109375 to 0.109375
- b_down: bfloat16 [2, 768], P('section', 'ctx'), may hold values from -2 to 2
Outputs:
- boundary_out: float32 [2, 4, 1024, 768], P('section', None, 'ctx')
- g_ln1_gain: float32 [2, 768], P('section', 'ctx')
- g_ln1_bias: float32 [2, 768], P('section', 'ctx')
- g_w_qkv: float32 [2, 3, 768, 768], P('section', None, 'ctx', 'tensor')
- g_b_qv: float32 [2, 2, 768], P('section', None, 'tensor')
- g_w_out: float32 [2, 768, 768], P('section', 'tensor', 'ctx')
- g_b_out: float32 [2, 768], P('section', 'ctx')
- g_ln2_gain: float32 [2, 768], P('section', 'ctx')
- g_ln2_bias: float32 [2, 768], P('section', 'ctx')
- g_w_up: float32 [2, 768, 3072], P('section', 'ctx', 'tensor')
- g_b_up: float32 [2, 3072], P('section', 'tensor')
- g_w_down: float32 [2, 3072, 768], P('section', 'tensor', 'ctx')
- g_b_down: float32 [2, 768], P('section', 'ctx')
The draws below stay inside these ranges and needn't reach their ends.
Inputs may be any that keep to these rules, and one draw needn't show every extreme that they name: `segments`: document numbers never fall along a sequence; every document has 1 to 512 tokens, and one has exactly 512.
All inputs are finite; a program needn't handle non-finite values.
Results may differ from the reference program's by a relative error of at most 0.03.
Values may be sent and summed in bfloat16 or wider, within the bound.
A program may use at most 192 MiB of HBM per device.

```python
import math
import jax
import jax.numpy as jnp
import numpy as np
from jax import lax

D = 768
HEADS = 12
HEAD = 64
FF = 3072
MB = 4
SEQ = 1024
N_SECTION = 2


def block_levels(stream_key, dims, cuts, smallest, high):
    def one(dim, blocks):
        heights = jax.random.uniform(jax.random.fold_in(jax.random.fold_in(stream_key, 6), dim), (blocks,), jnp.float32, smallest / len(cuts), high / len(cuts))
        return jnp.repeat(jnp.exp(heights), dims[dim] // blocks).reshape((-1,) + (1,) * (len(dims) - dim - 1))

    factor_of = one(*cuts[0])
    for cut in cuts[1:]:
        factor_of = factor_of * one(*cut)
    return factor_of


def length_profile(amount, total, bound, skew):
    weights = [(1 << 20) // math.isqrt(grade ** skew) + 1 for grade in range(2, amount + 1)]
    spare, counts = total - bound - (amount - 1), [1] * (amount - 1)
    while spare > 0:
        free = [i for i in range(amount - 1) if counts[i] < bound]
        mass, left = sum([weights[i] for i in free]), spare
        for i in free:
            more = min(bound - counts[i], max(1, left * weights[i] // mass), spare)
            counts[i] = counts[i] + more
            spare = spare - more
    return np.array([bound] + counts)


def ragged(own_key, count, total, reach, lean):
    if count == 2:
        one = jax.random.randint(own_key, (), max(1, total - reach), min(reach, total - 1) + 1)
        return jnp.stack([one, total - one])
    sizes = jnp.asarray(length_profile(count, total, reach, lean), jnp.int32)
    pairs = (count - 1) // 2
    source_of, taker = sizes[1:1 + 2 * pairs:2], sizes[2:2 + 2 * pairs:2]
    room = jnp.minimum(source_of - 1, reach - taker)
    moved = jax.random.randint(jax.random.fold_in(own_key, 1), (pairs,), 0, 1 << 20) % (room + 1)
    sizes = sizes.at[1:1 + 2 * pairs:2].set(source_of - moved).at[2:2 + 2 * pairs:2].set(taker + moved)
    return sizes[jax.random.permutation(jax.random.fold_in(own_key, 2), count)]


def scatter_about(rng, extent, deviation, most, shards=(), held_as=jnp.bfloat16):
    entries = deviation * jax.random.normal(rng, extent, jnp.float32)
    if shards:
        entries = entries * block_levels(rng, extent, shards, -0.22, 0.18)
    return jnp.clip(entries, -most, most).astype(held_as)


def setup_inputs(seed: int = 0) -> dict:
    keys = jax.random.split(jax.random.key(seed), 15)
    boundary_in = scatter_about(keys[0], (N_SECTION, MB, SEQ, D), 1.0, 6.0, ((0, 2), (2, 4)))
    segments = jax.vmap(lambda own: jnp.searchsorted(jnp.cumsum(ragged(own, max(3, SEQ // 512), SEQ, SEQ // 2, 2)), jnp.arange(SEQ), side="right"))(jax.random.split(keys[1], MB)).reshape((MB, SEQ)).astype(jnp.int32)
    ln1_gain = jnp.clip(1.0 + 0.1 * jax.random.normal(keys[2], (N_SECTION, D), jnp.float32), 0.5, 1.5).astype(jnp.bfloat16)
    ln1_bias = scatter_about(keys[3], (N_SECTION, D), 0.3, 2.0, ((0, 2), (1, 4)))
    w_qkv = scatter_about(keys[4], (N_SECTION, 3, D, D), D ** -0.5, 0.21875, ((0, 2), (2, 4), (3, 4)))
    b_qv = scatter_about(keys[5], (N_SECTION, 2, D), 0.05, 0.29882812, ((0, 2), (2, 4)))
    w_out = scatter_about(keys[6], (N_SECTION, D, D), 4 ** -0.5, 3.0, ((0, 2), (1, 4), (2, 4)))
    b_out = scatter_about(keys[7], (N_SECTION, D), 0.5, 3.0, ((0, 2), (1, 4)))
    ln2_gain = jnp.clip(1.0 + 0.1 * jax.random.normal(keys[8], (N_SECTION, D), jnp.float32), 0.5, 1.5).astype(jnp.bfloat16)
    ln2_bias = scatter_about(keys[9], (N_SECTION, D), 0.3, 2.0, ((0, 2), (1, 4)))
    w_up = scatter_about(keys[10], (N_SECTION, D, FF), D ** -0.5, 0.21875, ((0, 2), (1, 4), (2, 4)))
    b_up = scatter_about(keys[11], (N_SECTION, FF), 0.5, 3.0, ((0, 2), (1, 4)))
    w_down = scatter_about(keys[12], (N_SECTION, FF, D), FF ** -0.5, 0.109375, ((0, 2), (1, 4), (2, 4)))
    b_down = scatter_about(keys[13], (N_SECTION, D), 0.3, 2.0, ((0, 2), (1, 4)))
    return {"boundary_in": boundary_in, "segments": segments, "ln1_gain": ln1_gain, "ln1_bias": ln1_bias, "w_qkv": w_qkv, "b_qv": b_qv, "w_out": w_out, "b_out": b_out, "ln2_gain": ln2_gain, "ln2_bias": ln2_bias, "w_up": w_up, "b_up": b_up, "w_down": w_down, "b_down": b_down}


@jax.custom_vjp
def low(v):
    return lax.optimization_barrier(v.astype(jnp.bfloat16)).astype(jnp.float32)

@jax.custom_vjp
def low_back(v):
    return v

def low_keep(v):
    return (low(v), None)

def low_pass(kept, grad):
    return (grad,)

def back_keep(v):
    return (v, None)

def back_low(kept, grad):
    return (low(grad),)
low.defvjp(low_keep, low_pass)
low_back.defvjp(back_keep, back_low)
highest = lax.Precision.HIGHEST

def norm_rows(values_in, gain_vec, offset):
    average = lax.optimization_barrier(jnp.mean(values_in, axis=-1, keepdims=True))
    centered = values_in - average
    variance = lax.optimization_barrier(jnp.mean(centered * centered, axis=-1, keepdims=True))
    return centered * lax.rsqrt(variance + 1e-05) * gain_vec + offset

def attend(query_rows, key_rows, value_rows, seg_row):
    length = query_rows.shape[0]
    block_len = min(512, length)
    block_count = length // block_len
    positions = jnp.arange(length, dtype=jnp.int32)

    def one_block(members):
        block_query, block_pos, block_seg = members
        scores = low_back(jnp.einsum('qhd,khd->hqk', block_query, key_rows, precision=highest))
        allowed = (block_seg[:, None] == seg_row[None, :]) & (positions[None, :] <= block_pos[:, None])
        scores = jnp.where(allowed[None], scores, -1e+30)
        row_max = lax.optimization_barrier(jnp.max(scores, axis=-1, keepdims=True))
        expweights = jnp.where(allowed[None], jnp.exp(scores - row_max), 0.0)
        log_total = row_max + jnp.log(lax.optimization_barrier(jnp.sum(expweights, axis=-1, keepdims=True)))
        normalized = low(jnp.where(allowed[None], jnp.exp(scores - log_total), 0.0))
        return jnp.einsum('hqk,khd->qhd', normalized, value_rows, precision=highest)
    result = lax.map(jax.checkpoint(one_block), (query_rows.reshape(block_count, block_len, HEADS, HEAD), positions.reshape(block_count, block_len), seg_row.reshape(block_count, block_len)))
    return result.reshape(length, HEADS * HEAD)

def layer(values_in, seg_row, params):
    normed = low(norm_rows(values_in, params[0], params[1]))
    projected = jnp.einsum('td,cde->cte', normed, params[2], precision=highest)
    scale = 1.0 / math.sqrt(HEAD)
    query_rows = low_back(low((projected[0] + params[3][0]) * scale))
    key_rows = low_back(low(projected[1]))
    value_rows = low_back(low(projected[2] + params[3][1]))
    shape = (values_in.shape[0], HEADS, HEAD)
    attended = attend(query_rows.reshape(shape), key_rows.reshape(shape), value_rows.reshape(shape), seg_row)
    attended = low_back(low(attended))
    branch = low_back(jnp.dot(attended, params[4], precision=highest) + params[5])
    middle = values_in + branch
    normed_two = low(norm_rows(middle, params[6], params[7]))
    raised = low_back(jnp.dot(normed_two, params[8], precision=highest) + params[9])
    active = low(jax.nn.gelu(raised, approximate=True))
    lowered = low_back(jnp.dot(active, params[10], precision=highest) + params[11])
    return middle + lowered

def reference(boundary_in, segments, ln1_gain, ln1_bias, w_qkv, b_qv, w_out, b_out, ln2_gain, ln2_bias, w_up, b_up, w_down, b_down):
    weights = tuple((member.astype(jnp.float32) for member in (ln1_gain, ln1_bias, w_qkv, b_qv, w_out, b_out, ln2_gain, ln2_bias, w_up, b_up, w_down, b_down)))
    inputs = boundary_in[0].astype(jnp.float32)
    cotangent = boundary_in[1].astype(jnp.float32)

    def forward(first_in, params):
        lower = tuple((member[0] for member in params))
        upper = tuple((member[1] for member in params))
        results = []
        for batch_index in range(MB):
            passed = low_back(low(layer(first_in[batch_index], segments[batch_index], lower)))
            results.append(layer(passed, segments[batch_index], upper))
        return jnp.stack(results)
    result, pull = jax.vjp(forward, inputs, weights)
    grad_in, grads = pull(cotangent)
    return (jnp.stack([grad_in, result]), grads[0], grads[1], grads[2], grads[3], grads[4], grads[5], grads[6], grads[7], grads[8], grads[9], grads[10], grads[11])
```

```python
import math

import jax
import jax.numpy as jnp
from jax import lax
from jax.sharding import PartitionSpec as P

HEAD = 64
NORM_EPS = 1e-05
NEG_BIG = -1e30
BF = jnp.bfloat16
F32 = jnp.float32
ROWS = ("tensor", "ctx")


def norm_parts(x, gain, shift):
    mean = jnp.mean(x, axis=-1, keepdims=True)
    centered = x - mean
    inverse = lax.rsqrt(jnp.mean(centered * centered, axis=-1, keepdims=True) + NORM_EPS)
    normal = centered * inverse
    return normal * gain + shift, normal, inverse


def norm_back(upstream, normal, inverse, gain):
    scaled = upstream * gain
    return inverse * (
        scaled
        - jnp.mean(scaled, axis=-1, keepdims=True)
        - normal * jnp.mean(scaled * normal, axis=-1, keepdims=True)
    )


def act(u):
    return jax.nn.gelu(u, approximate=True)


def dot(spec, a, b):
    return jnp.einsum(spec, a, b, preferred_element_type=F32)


def heads(a):
    return a.reshape(a.shape[0], a.shape[1], a.shape[2] // HEAD, HEAD)


def attend(q, k, v, allowed):
    scores = jnp.where(allowed, dot("tnhd,tmhd->thnm", heads(q), heads(k)), NEG_BIG)
    top = jnp.max(scores, axis=-1, keepdims=True)
    total = jnp.sum(jnp.where(allowed, jnp.exp(scores - top), 0.0), axis=-1, keepdims=True)
    lse = top + jnp.log(total)
    chances = jnp.where(allowed, jnp.exp(scores - lse), 0.0).astype(BF)
    out = dot("thnm,tmhd->tnhd", chances, heads(v))
    return out.reshape(q.shape).astype(BF), lse


def attend_back(q, k, v, lse, allowed, d_out):
    scores = dot("tnhd,tmhd->thnm", heads(q), heads(k))
    chances = jnp.where(allowed, jnp.exp(scores - lse), 0.0)
    d_chance = dot("tnhd,tmhd->thnm", heads(d_out), heads(v))
    delta = jnp.sum(chances * d_chance, axis=-1, keepdims=True)
    d_score = (chances * (d_chance - delta)).astype(BF)
    d_v = dot("thnm,tnhd->tmhd", chances.astype(BF), heads(d_out))
    d_k = dot("thnm,tnhd->tmhd", d_score, heads(q))
    d_q = dot("thnm,tmhd->tnhd", d_score, heads(k))
    return d_q.reshape(q.shape), d_k.reshape(k.shape), d_v.reshape(v.shape)


def forward(x_ctx, weights, vecs, allowed):
    w_attn, w_mlp = weights
    part = w_attn.shape[2] // 4
    hidden = w_mlp.shape[2] // 2
    bias_q, bias_v, bias_up, ln1_g, ln1_b, bias_out, ln2_g, ln2_b, bias_down = vecs
    rows = allowed.shape[0]
    h_ctx, normal_ctx, inverse_ctx = norm_parts(x_ctx.astype(F32), ln1_g, ln1_b)
    h_ctx = h_ctx.astype(BF)
    x = x_ctx[-rows:].astype(F32)
    q = (dot("nd,tdk->tnk", h_ctx[-rows:], w_attn[:, :, :part]) + bias_q) / math.sqrt(HEAD)
    q = q.astype(BF)
    k = dot("nd,tdk->tnk", h_ctx, w_attn[:, :, part : 2 * part]).astype(BF)
    v = (dot("nd,tdk->tnk", h_ctx, w_attn[:, :, 2 * part : 3 * part]) + bias_v).astype(BF)
    o, lse = attend(q, k, v, allowed)
    middle = x + dot("tnk,tdk->nd", o, w_attn[:, :, 3 * part :]) + bias_out
    h2, normal2, inverse2 = norm_parts(middle, ln2_g, ln2_b)
    h2 = h2.astype(BF)
    raised = dot("nd,tdf->tnf", h2, w_mlp[:, :, :hidden]) + bias_up
    active = act(raised).astype(BF)
    y = middle + dot("tnf,tdf->nd", active, w_mlp[:, :, hidden:]) + bias_down
    saved = (
        h_ctx,
        normal_ctx[-rows:],
        inverse_ctx[-rows:],
        q,
        k,
        v,
        o,
        lse,
        h2,
        normal2,
        inverse2,
        raised,
        active,
    )
    return y, saved


def send_back(d_ctx, rows, window):
    total = d_ctx[-rows:]
    count = lax.axis_size("ctx")
    low = d_ctx[:-rows].astype(BF)
    for step in range(1, window + 1):
        start = (window - step) * rows
        total = total + lax.ppermute(
            low[start : start + rows], "ctx", [(i, i - step) for i in range(step, count)]
        ).astype(F32)
    return total


def backward(upstream, saved, weights, vecs, allowed, window, want_grads):
    w_attn, w_mlp = weights
    part = w_attn.shape[2] // 4
    hidden = w_mlp.shape[2] // 2
    ln1_g, ln2_g = vecs[3], vecs[6]
    h_ctx, normal1, inverse1, q, k, v, o, lse, h2, normal2, inverse2, raised, active = saved
    rows = allowed.shape[0]
    up_low = upstream.astype(BF)
    d_active = dot("nd,tdf->tnf", up_low, w_mlp[:, :, hidden:])
    d_raised = jax.vjp(act, raised)[1](d_active)[0].astype(BF)
    d_h2 = dot("tnf,tdf->nd", d_raised, w_mlp[:, :, :hidden])
    d_mid = upstream + norm_back(d_h2, normal2, inverse2, ln2_g)
    d_branch = d_mid.astype(BF)
    d_out = dot("nd,tdk->tnk", d_branch, w_attn[:, :, 3 * part :]).astype(BF)
    d_q, d_k, d_v = attend_back(q, k, v, lse, allowed, d_out)
    d_q = d_q.astype(BF) / math.sqrt(HEAD)
    d_k = d_k.astype(BF)
    d_v = d_v.astype(BF)
    d_ctx = dot("tnk,tdk->nd", d_k, w_attn[:, :, part : 2 * part]) + dot(
        "tnk,tdk->nd", d_v, w_attn[:, :, 2 * part : 3 * part]
    )
    d_own = dot("tnk,tdk->nd", d_q, w_attn[:, :, :part])
    d_h = send_back(d_ctx, rows, window) + d_own
    d_x = d_mid + norm_back(d_h, normal1, inverse1, ln1_g)
    if not want_grads:
        return d_x
    mlp_grad = jnp.concatenate(
        [
            dot("nd,tnf->tdf", h2, d_raised).astype(BF),
            dot("nd,tnf->tdf", up_low, active).astype(BF),
        ],
        axis=2,
    )
    attn_grad = jnp.concatenate(
        [
            dot("nd,tnk->tdk", h_ctx[-rows:], d_q).astype(BF),
            dot("nd,tnk->tdk", h_ctx, d_k).astype(BF),
            dot("nd,tnk->tdk", h_ctx, d_v).astype(BF),
            dot("nd,tnk->tdk", d_branch, o).astype(BF),
        ],
        axis=2,
    )
    flat = [
        jnp.sum(d_h * normal1, axis=0),
        jnp.sum(d_h, axis=0),
        jnp.sum(d_branch.astype(F32), axis=0),
        jnp.sum(d_h2 * normal2, axis=0),
        jnp.sum(d_h2, axis=0),
        jnp.sum(up_low.astype(F32), axis=0),
        jnp.sum(d_q.astype(F32), axis=1).reshape(-1),
        jnp.sum(d_v.astype(F32), axis=1).reshape(-1),
        jnp.sum(d_raised.astype(F32), axis=1).reshape(-1),
    ]
    return d_x, mlp_grad, attn_grad, jnp.concatenate(flat)


def local(
    boundary_in,
    segments,
    ln1_gain,
    ln1_bias,
    w_qkv,
    b_qv,
    w_out,
    b_out,
    ln2_gain,
    ln2_bias,
    w_up,
    b_up,
    w_down,
    b_down,
):
    section = lax.axis_index("section")
    ctx = lax.axis_index("ctx")
    tensor = lax.axis_index("tensor")
    n_ctx = lax.axis_size("ctx")
    n_tensor = lax.axis_size("tensor")
    rows = boundary_in.shape[2]
    seq = segments.shape[1]
    own_d, part = w_out.shape[2], w_out.shape[1]
    hidden = w_up.shape[2]
    width = own_d * n_ctx
    window = min(n_ctx - 1, (seq // 2 - 1 + rows - 1) // rows)

    x_own = lax.dynamic_index_in_dim(boundary_in[0], tensor, 0, keepdims=False)
    x_blocks = [
        lax.ppermute(x_own, "ctx", [(i, i + step) for i in range(n_ctx - step)])
        for step in range(window, 0, -1)
    ] + [x_own]

    vec_own = jnp.concatenate(
        [
            b_up[0],
            b_qv[0].reshape(-1),
            ln1_gain[0],
            ln1_bias[0],
            b_out[0],
            ln2_gain[0],
            ln2_bias[0],
            b_down[0],
        ]
    )
    vec_all = lax.all_gather(vec_own[None], ROWS, axis=0, tiled=True).astype(F32)
    vec_all = vec_all.reshape(n_tensor, n_ctx, -1)
    attn_own = jnp.concatenate(
        [jnp.transpose(w_qkv[0], (1, 0, 2)).reshape(own_d, 3 * part), jnp.transpose(w_out[0])], axis=1
    )
    mlp_own = jnp.concatenate([w_up[0], jnp.transpose(w_down[0])], axis=1)
    w_attn = lax.all_gather(attn_own, ROWS, axis=0, tiled=True).reshape(n_tensor, width, -1)
    w_mlp = lax.all_gather(mlp_own, ROWS, axis=0, tiled=True).reshape(n_tensor, width, -1)
    weights = (w_attn, w_mlp)
    per_tensor = vec_all[:, 0, :, None]
    bias_up = per_tensor[:, :hidden].reshape(n_tensor, 1, hidden)
    bias_q = per_tensor[:, hidden : hidden + part].reshape(n_tensor, 1, part)
    bias_v = per_tensor[:, hidden + part : hidden + 2 * part].reshape(n_tensor, 1, part)
    wide = vec_all[0, :, hidden + 2 * part :].reshape(n_ctx, 6, own_d)
    wide = jnp.transpose(wide, (1, 0, 2)).reshape(6, width)
    vecs = (bias_q, bias_v, bias_up) + tuple(wide[i] for i in range(6))

    seg = lax.dynamic_index_in_dim(segments, tensor, 0, keepdims=False)
    seg_pad = jnp.concatenate([jnp.full((window * rows,), -1, jnp.int32), seg])
    seg_keys = lax.dynamic_slice_in_dim(seg_pad, ctx * rows, (window + 1) * rows)
    seg_rows = seg_keys[-rows:]
    key_pos = jnp.arange((window + 1) * rows, dtype=jnp.int32) - window * rows
    row_pos = jnp.arange(rows, dtype=jnp.int32)
    allowed = (seg_rows[:, None] == seg_keys[None, :]) & (key_pos[None, :] <= row_pos[:, None])

    first, unused = forward(jnp.concatenate(x_blocks), weights, vecs, allowed)
    first_low = first.astype(BF)
    passed = [
        lax.ppermute(
            first_low,
            ("section", "ctx"),
            [(i, n_ctx + i + step) for i in range(n_ctx - step)],
        )
        for step in range(window, -1, -1)
    ]
    chosen = [jnp.where(section == 0, a, b) for a, b in zip(x_blocks, passed)]
    result, saved = forward(jnp.concatenate(chosen), weights, vecs, allowed)

    upper = backward(x_own.astype(F32), saved, weights, vecs, allowed, window, False)
    returned = lax.ppermute(upper.astype(BF), "section", [(1, 0)])
    upstream = jnp.where(section == 0, returned, x_own).astype(F32)
    d_x, mlp_grad, attn_grad, flat = backward(
        upstream, saved, weights, vecs, allowed, window, True
    )

    mlp_sum = lax.psum_scatter(
        mlp_grad.reshape(n_tensor * width, -1), ROWS, scatter_dimension=0, tiled=True
    ).astype(F32)
    attn_sum = lax.psum_scatter(
        attn_grad.reshape(n_tensor * width, -1), ROWS, scatter_dimension=0, tiled=True
    ).astype(F32)
    flat = lax.psum(flat, ROWS)
    ends = lax.all_gather(
        jnp.where(section == 0, d_x, result).astype(BF), "tensor", axis=0
    ).astype(F32)

    wide_sum = lax.dynamic_slice_in_dim(flat[: 6 * width].reshape(6, width), ctx * own_d, own_d, 1)
    qv_sum = flat[6 * width : 6 * width + 2 * n_tensor * part].reshape(2, n_tensor, part)
    qv_sum = lax.dynamic_index_in_dim(qv_sum, tensor, 1, keepdims=False)
    up_sum = flat[6 * width + 2 * n_tensor * part :].reshape(n_tensor, hidden)
    up_sum = lax.dynamic_index_in_dim(up_sum, tensor, 0, keepdims=False)
    g_qkv = jnp.transpose(attn_sum[:, : 3 * part].reshape(own_d, 3, part), (1, 0, 2))
    g_out = jnp.transpose(attn_sum[:, 3 * part :])
    g_up = mlp_sum[:, :hidden]
    g_down = jnp.transpose(mlp_sum[:, hidden:])
    return (
        ends[None],
        wide_sum[0][None],
        wide_sum[1][None],
        g_qkv[None],
        qv_sum[None],
        g_out[None],
        wide_sum[2][None],
        wide_sum[3][None],
        wide_sum[4][None],
        g_up[None],
        up_sum[None],
        g_down[None],
        wide_sum[5][None],
    )


def solution(mesh):
    in_specs = (
        P("section", None, "ctx", None),
        P(),
        P("section", "ctx"),
        P("section", "ctx"),
        P("section", None, "ctx", "tensor"),
        P("section", None, "tensor"),
        P("section", "tensor", "ctx"),
        P("section", "ctx"),
        P("section", "ctx"),
        P("section", "ctx"),
        P("section", "ctx", "tensor"),
        P("section", "tensor"),
        P("section", "tensor", "ctx"),
        P("section", "ctx"),
    )
    out_specs = (
        P("section", None, "ctx", None),
        P("section", "ctx"),
        P("section", "ctx"),
        P("section", None, "ctx", "tensor"),
        P("section", None, "tensor"),
        P("section", "tensor", "ctx"),
        P("section", "ctx"),
        P("section", "ctx"),
        P("section", "ctx"),
        P("section", "ctx", "tensor"),
        P("section", "tensor"),
        P("section", "tensor", "ctx"),
        P("section", "ctx"),
    )
    return jax.shard_map(local, mesh=mesh, in_specs=in_specs, out_specs=out_specs, check_vma=False)
```
